128 devices in a mesh: gx: 4 (over x), yz: 32 (over y, z, core).
Axes of the slice: x: 4, y: 4, z: 4, core: 2. Of those that a mesh axis runs over, the one named last changes fastest.
Arguments:
- tokens: bfloat16 [512, 12288], P(None, ('gx', 'yz')), may hold values from -24 to 24
- gate_weight: bfloat16 [12288, 40960], P('gx', 'yz'), may hold values from -0.0546875 to 0.0546875
- up_weight: bfloat16 [12288, 40960], P('gx', 'yz'), may hold values from -0.0546875 to 0.0546875
- down_weight: bfloat16 [40960, 12288], P('yz', 'gx'), may hold values from -0.0546875 to 0.0546875
Outputs:
- mixed: bfloat16 [512, 12288], P(None, ('gx', 'yz'))
The draws below stay inside these ranges and needn't reach their ends.
All inputs are finite; a program needn't handle non-finite values.
Results may differ from the reference program's by a relative error of at most 0.0049.
Values may be sent and summed in bfloat16 or wider, within the bound.
A program may use at most 128 MiB of HBM per device.

```python
import jax
import jax.numpy as jnp

D = 12288
FF = 40960
TOKENS = 512


def with_spikes(result, stream_key, source, target, shards_of, factor):
    def block_of(dim):
        return (jnp.arange(result.shape[dim]) // (result.shape[dim] // shards_of)).reshape((-1,) + (1,) * (result.ndim - 1 - dim))

    first = jax.random.permutation(stream_key, shards_of)[block_of(target)]
    far = (block_of(target) + shards_of // 2) % shards_of
    return jnp.where((block_of(source) == first) | (block_of(source) == far), factor * result, result)


def block_levels(own_key, dims, cuts, low, top_value):
    def one(axis_at, shards_of):
        heights = jax.random.uniform(jax.random.fold_in(jax.random.fold_in(own_key, 6), axis_at), (shards_of,), jnp.float32, low / len(cuts), top_value / len(cuts))
        return jnp.repeat(jnp.exp(heights), dims[axis_at] // shards_of).reshape((-1,) + (1,) * (len(dims) - axis_at - 1))

    factor_of = one(*cuts[0])
    for cut in cuts[1:]:
        factor_of = factor_of * one(*cut)
    return factor_of


def gaussian(rng, extent, scale, reach, split=(), kind=jnp.bfloat16):
    drawn = jax.random.normal(rng, extent, jnp.float32) * scale
    if len(split) > 0:
        drawn = block_levels(rng, extent, split, -0.22, 0.18) * drawn
    return jnp.clip(drawn, min=-reach, max=reach).astype(kind)


def heavy_noise(rng, shape, deviation, reach, cuts, heavy, dtype=jnp.bfloat16):
    values = deviation * jax.random.normal(rng, shape, jnp.float32)
    if cuts:
        values = values * block_levels(rng, shape, cuts, -0.22, 0.18)
    return jnp.clip(with_spikes(values, jax.random.fold_in(rng, 3), *heavy), -reach, reach).astype(dtype)


def setup_inputs(seed: int = 0) -> dict:
    arg_keys = jax.random.split(jax.random.key(seed), 5)
    tokens = heavy_noise(arg_keys[0], (TOKENS, D), 1.0, 24.0, ((1, 128),), (1, 0, 128, 5.5))
    gate_weight = gaussian(arg_keys[1], (D, FF), D ** -0.5, 0.0546875, ((0, 4), (1, 32)))
    up_weight = gaussian(arg_keys[2], (D, FF), D ** -0.5, 0.0546875, ((0, 4), (1, 32)))
    down_weight = heavy_noise(arg_keys[3], (FF, D), FF ** -0.5, 0.0546875, ((0, 32), (1, 4)), (0, 1, 32, 2.75))
    return dict(tokens=tokens, gate_weight=gate_weight, up_weight=up_weight, down_weight=down_weight)


def reference(tokens, gate_weight, up_weight, down_weight):
    gate = jnp.dot(tokens, gate_weight, preferred_element_type=jnp.float32)
    up = jnp.dot(tokens, up_weight, preferred_element_type=jnp.float32)
    hidden = (jax.nn.silu(gate) * up).astype(jnp.bfloat16)
    return jnp.dot(hidden, down_weight, preferred_element_type=jnp.float32).astype(jnp.bfloat16)
```

```python
import jax
import jax.numpy as jnp
from jax import lax
from jax.experimental import pallas as pl
from jax.experimental.pallas import tpu as pltpu
from jax.sharding import PartitionSpec as P

MESH = pl.DeviceIdType.MESH
F32 = jnp.float32
BF16 = jnp.bfloat16

TOK = 512
NC = 4
T = TOK // NC
Q = T // 4
DL = 3072
FL = 1280
NB = 96
CH = 16


def kernel(tok, wg_h, wu_h, wd_h, out,
           wg, wu, wd, xt, xn, pg, pu, sg, su, r1g, r1u, mg, mu, rmg, rmu, rpg, rpu,
           hb, ob, of, sib, sd, sf, rd,
           wsem, a_s, a_r, as_s, as_r, x_s, x_r, d0_s, d0_r, d1_s, d1_r):
    x = lax.axis_index("gx")
    yz = lax.axis_index("yz")
    chip = yz // 2
    k = yz % 2
    y = chip // 4
    z = chip % 4
    xp = (x + 1) % 4
    xm = (x + 3) % 4
    xo = (x + 2) % 4
    sibling = (x, chip * 2 + (1 - k))
    plus = (xp, yz)
    minus = (xm, yz)

    def peer(o):
        return ((y + o // 4) % 4) * 4 + (z + o % 4) % 4

    weights = [pltpu.make_async_copy(h, v, wsem.at[i]) for i, (h, v) in enumerate(((wg_h, wg), (wu_h, wu), (wd_h, wd)))]
    for w in weights:
        w.start()

    barrier = pltpu.get_barrier_semaphore()

    def greet(o, _):
        pl.semaphore_signal(barrier, inc=1, device_id=(x, peer(o) * 2 + k), device_id_type=MESH)
        return 0

    lax.fori_loop(1, CH, greet, 0)
    for dev in (sibling, plus, minus):
        pl.semaphore_signal(barrier, inc=1, device_id=dev, device_id_type=MESH)

    for c in range(NC):
        xt[c, chip, k] = tok[c * T:(c + 1) * T, :].astype(F32).T.astype(BF16)

    pl.semaphore_wait(barrier, CH - 1 + 3)

    def rcopy(src, dst, ss, rs, dev):
        return pltpu.make_async_remote_copy(src_ref=src, dst_ref=dst, send_sem=ss, recv_sem=rs,
                                            device_id=dev, device_id_type=MESH)

    def a_send(c):
        def one(o, _):
            own = xt.at[c, chip, k]
            rcopy(own, own, a_s.at[c], a_r.at[c], (x, peer(o) * 2 + k)).start()
            return 0
        lax.fori_loop(1, CH, one, 0)

    def a_all(c):
        ref = xt.at[c, pl.ds(0, CH - 1), k]
        return rcopy(ref, ref, a_s.at[c], a_r.at[c], sibling)

    def a_pass(c):
        ref = xt.at[c, :, k]
        return rcopy(ref, ref, as_s.at[c], as_r.at[c], sibling)

    def x_copy(c, i):
        table = (
            (sg.at[c, xo], r1g.at[c], plus),
            (sg.at[c, xm], rpg.at[c], minus),
            (su.at[c, xp], rmu.at[c], plus),
            (su.at[c, xo], r1u.at[c], minus),
            (mg.at[c], rmg.at[c], plus),
            (mu.at[c], rpu.at[c], minus),
            (hb.at[c, x], hb.at[c, x], plus),
            (hb.at[c, x], hb.at[c, x], minus),
            (hb.at[c, xm, pl.ds(0, Q // 2)], hb.at[c, xm, pl.ds(0, Q // 2)], plus),
            (hb.at[c, xp, pl.ds(Q // 2, Q // 2)], hb.at[c, xp, pl.ds(Q // 2, Q // 2)], minus),
        )
        src, dst, dev = table[i]
        return rcopy(src, dst, x_s.at[c, i], x_r.at[c, i], dev)

    def x_recv(c, i):
        dst = (r1g.at[c], rpg.at[c], rmu.at[c], r1u.at[c], rmg.at[c], rpu.at[c],
               hb.at[c, xm], hb.at[c, xp],
               hb.at[c, xo, pl.ds(0, Q // 2)], hb.at[c, xo, pl.ds(Q // 2, Q // 2)])[i]
        rcopy(dst, dst, x_s.at[c, i], x_r.at[c, i], plus).wait_recv()

    def m1(c):
        a_all(c).wait_recv()
        a_pass(c).start()
        if c + 1 < NC:
            a_send(c + 1)
        if c == 0:
            weights[0].wait()
        a_in = xt.at[c, :, 1 - k]
        rcopy(a_in, a_in, as_s.at[c], as_r.at[c], sibling).wait_recv()
        for j in range(8):
            blk = xt[c, 2 * j:2 * j + 2].reshape(384, T)
            xn[:, 384 * j:384 * (j + 1)] = blk.astype(F32).T.astype(BF16)

        def half(w, pf, sb):
            @pl.loop(0, FL // 256)
            def _(j):
                cols = pl.ds(pl.multiple_of(j * 256, 256), 256)
                r = jnp.dot(xn[...], w[:, cols], preferred_element_type=F32)
                pf[c, :, cols] = r
                sb[c, :, :, cols] = r.astype(BF16).reshape(4, Q, 256)

        half(wg, pg, sg)
        x_copy(c, 0).start()
        x_copy(c, 1).start()
        if c == 0:
            weights[1].wait()
        half(wu, pu, su)
        x_copy(c, 2).start()
        x_copy(c, 3).start()

    def rows(q):
        return pl.ds(pl.multiple_of(q * Q, Q), Q)

    def relay(c):
        x_recv(c, 0)
        mg[c] = (pg[c, rows(xp), :] + r1g[c].astype(F32)).astype(BF16)
        x_copy(c, 4).start()
        x_recv(c, 3)
        mu[c] = (pu[c, rows(xm), :] + r1u[c].astype(F32)).astype(BF16)
        x_copy(c, 5).start()

    def act(c):
        x_recv(c, 1)
        x_recv(c, 2)
        x_recv(c, 4)
        x_recv(c, 5)
        gate = pg[c, rows(x), :] + rmg[c].astype(F32) + rpg[c].astype(F32)
        up = pu[c, rows(x), :] + rmu[c].astype(F32) + rpu[c].astype(F32)
        hb[c, x] = (gate / (1.0 + jnp.exp(-gate)) * up).astype(BF16)
        x_copy(c, 6).start()
        x_copy(c, 7).start()

    def forward(c):
        x_recv(c, 6)
        x_copy(c, 8).start()
        x_recv(c, 7)
        x_copy(c, 9).start()

    def d0(c):
        return rcopy(ob.at[c, :, 1 - k], sib.at[c], d0_s.at[c], d0_r.at[c], sibling)

    def m2(c):
        x_recv(c, 8)
        x_recv(c, 9)
        if c == 0:
            weights[2].wait()

        @pl.loop(0, 8)
        def _(j):
            cols = pl.ds(pl.multiple_of(j * 384, 384), 384)
            r = jnp.dot(hb[c].reshape(T, FL), wd[:, cols], preferred_element_type=F32)
            r = r.T
            of[pl.ds(2 * j, 2)] = r.reshape(2, 2, NB, T)
            ob[c, pl.ds(2 * j, 2)] = r.astype(BF16).reshape(2, 2, NB, T)

        d0(c).start()
        d0(c).wait_recv()
        s = of[:, k] + sib[c].astype(F32)
        sd[c] = s.astype(BF16)
        sf[c] = of[chip, k] + sib[c, chip].astype(F32)

        def one(o, _):
            q = peer(o)
            rcopy(sd.at[c, q], rd.at[c, o - 1], d1_s.at[c], d1_r.at[c], (x, q * 2 + k)).start()
            return 0
        lax.fori_loop(1, CH, one, 0)

    def d1_all(c):
        return rcopy(rd.at[c], rd.at[c], d1_s.at[c], d1_r.at[c], sibling)

    def finish(c):
        d1_all(c).wait_recv()
        total = sf[c]
        for o in range(CH - 1):
            total = total + rd[c, o].astype(F32)
        out[c * T:(c + 1) * T, :] = total.T.astype(BF16)

    a_send(0)
    for s in range(NC + 5):
        for off, step in ((0, m1), (1, relay), (2, act), (3, forward), (3, m2), (4, finish)):
            if 0 <= s - off < NC:
                step(s - off)

    for c in range(NC):
        a_all(c).wait_send()
        a_pass(c).wait_send()
        for i in range(10):
            x_copy(c, i).wait_send()
        d0(c).wait_send()
        d1_all(c).wait_send()


def body(tokens, gate_weight, up_weight, down_weight):
    vm = pltpu.VMEM
    dma = pltpu.SemaphoreType.DMA
    return pl.pallas_call(
        kernel,
        out_shape=jax.ShapeDtypeStruct((TOK, NB), BF16),
        in_specs=[pl.BlockSpec(memory_space=pltpu.VMEM)] + [pl.BlockSpec(memory_space=pl.ANY)] * 3,
        out_specs=pl.BlockSpec(memory_space=pltpu.VMEM),
        scratch_shapes=[
            vm((DL, FL), BF16), vm((DL, FL), BF16), vm((FL, DL), BF16),
            vm((NC, CH, 2, NB, T), BF16), vm((T, DL), BF16),
            vm((NC, T, FL), F32), vm((NC, T, FL), F32),
            vm((NC, 4, Q, FL), BF16), vm((NC, 4, Q, FL), BF16),
            vm((NC, Q, FL), BF16), vm((NC, Q, FL), BF16),
            vm((NC, Q, FL), BF16), vm((NC, Q, FL), BF16),
            vm((NC, Q, FL), BF16), vm((NC, Q, FL), BF16),
            vm((NC, Q, FL), BF16), vm((NC, Q, FL), BF16),
            vm((NC, 4, Q, FL), BF16),
            vm((NC, CH, 2, NB, T), BF16), vm((CH, 2, NB, T), F32),
            vm((NC, CH, NB, T), BF16), vm((NC, CH, NB, T), BF16),
            vm((NC, NB, T), F32), vm((NC, CH - 1, NB, T), BF16),
            dma((3,)), dma((NC,)), dma((NC,)), dma((NC,)), dma((NC,)),
            dma((NC, 10)), dma((NC, 10)), dma((NC,)), dma((NC,)), dma((NC,)), dma((NC,)),
        ],
        compiler_params=pltpu.CompilerParams(
            collective_id=0, has_side_effects=True, vmem_limit_bytes=60 * 2 ** 20
        ),
        cost_estimate=pl.CostEstimate(flops=12 * 10 ** 9, bytes_accessed=24 * 10 ** 6, transcendentals=0),
    )(tokens, gate_weight, up_weight, down_weight)


def solution(mesh):
    return jax.shard_map(
        body,
        mesh=mesh,
        in_specs=(P(None, ("gx", "yz")), P("gx", "yz"), P("gx", "yz"), P("yz", "gx")),
        out_specs=P(None, ("gx", "yz")),
        check_vma=False,
    )
```

```python
import jax
import jax.numpy as jnp
from jax import lax
from jax.experimental import pallas as pl
from jax.experimental.pallas import tpu as pltpu
from jax.sharding import PartitionSpec as P

MESH = pl.DeviceIdType.MESH
F32 = jnp.float32
BF16 = jnp.bfloat16

TOK = 512
NC = 4
T = TOK // NC
Q = T // 4
DL = 3072
FL = 1280
NB = 96
CH = 16


def kernel(tok, wg_h, wu_h, wd_h, out,
           wg, wu, wd, xt, pg, pu, sg, su, r1g, r1u, mg, mu, rmg, rmu, rpg, rpu,
           hb, ob, of, sib, sd, sf, rd,
           wsem, a_s, a_r, as_s, as_r, x_s, x_r, d0_s, d0_r, d1_s, d1_r):
    x = lax.axis_index("gx")
    yz = lax.axis_index("yz")
    chip = yz // 2
    k = yz % 2
    y = chip // 4
    z = chip % 4
    xp = (x + 1) % 4
    xm = (x + 3) % 4
    xo = (x + 2) % 4
    sibling = (x, chip * 2 + (1 - k))
    plus = (xp, yz)
    minus = (xm, yz)

    def peer(o):
        return ((y + o // 4) % 4) * 4 + (z + o % 4) % 4

    weights = [pltpu.make_async_copy(h, v, wsem.at[i]) for i, (h, v) in enumerate(((wg_h, wg), (wu_h, wu), (wd_h, wd)))]
    for w in weights:
        w.start()

    barrier = pltpu.get_barrier_semaphore()

    def greet(o, _):
        pl.semaphore_signal(barrier, inc=1, device_id=(x, peer(o) * 2 + k), device_id_type=MESH)
        return 0

    lax.fori_loop(1, CH, greet, 0)
    for dev in (sibling, plus, minus):
        pl.semaphore_signal(barrier, inc=1, device_id=dev, device_id_type=MESH)

    for c in range(NC):
        xt[c, chip, k] = tok[:, c * T:(c + 1) * T]

    pl.semaphore_wait(barrier, CH - 1 + 3)

    def rcopy(src, dst, ss, rs, dev):
        return pltpu.make_async_remote_copy(src_ref=src, dst_ref=dst, send_sem=ss, recv_sem=rs,
                                            device_id=dev, device_id_type=MESH)

    def a_send(c):
        def one(o, _):
            own = xt.at[c, chip, k]
            rcopy(own, own, a_s.at[c], a_r.at[c], (x, peer(o) * 2 + k)).start()
            return 0
        lax.fori_loop(1, CH, one, 0)

    def a_all(c):
        ref = xt.at[c, pl.ds(0, CH - 1), k]
        return rcopy(ref, ref, a_s.at[c], a_r.at[c], sibling)

    def a_pass(c):
        ref = xt.at[c, :, k]
        return rcopy(ref, ref, as_s.at[c], as_r.at[c], sibling)

    def x_copy(c, i):
        table = (
            (sg.at[c, xo], r1g.at[c], plus),
            (sg.at[c, xm], rpg.at[c], minus),
            (su.at[c, xp], rmu.at[c], plus),
            (su.at[c, xo], r1u.at[c], minus),
            (mg.at[c], rmg.at[c], plus),
            (mu.at[c], rpu.at[c], minus),
            (hb.at[c, x], hb.at[c, x], plus),
            (hb.at[c, x], hb.at[c, x], minus),
            (hb.at[c, xm, pl.ds(0, Q // 2)], hb.at[c, xm, pl.ds(0, Q // 2)], plus),
            (hb.at[c, xp, pl.ds(Q // 2, Q // 2)], hb.at[c, xp, pl.ds(Q // 2, Q // 2)], minus),
        )
        src, dst, dev = table[i]
        return rcopy(src, dst, x_s.at[c, i], x_r.at[c, i], dev)

    def x_recv(c, i):
        dst = (r1g.at[c], rpg.at[c], rmu.at[c], r1u.at[c], rmg.at[c], rpu.at[c],
               hb.at[c, xm], hb.at[c, xp],
               hb.at[c, xo, pl.ds(0, Q // 2)], hb.at[c, xo, pl.ds(Q // 2, Q // 2)])[i]
        rcopy(dst, dst, x_s.at[c, i], x_r.at[c, i], plus).wait_recv()

    def to_sibling(c):
        a_all(c).wait_recv()
        a_pass(c).start()

    def dot_in(c, w, pf, sb):
        r = lax.dot_general(xt[c].reshape(DL, T), w[...], (((0,), (0,)), ((), ())), preferred_element_type=F32)
        pf[c] = r
        sb[c] = r.astype(BF16).reshape(4, Q, FL)

    def m_gate(c):
        a_in = xt.at[c, :, 1 - k]
        rcopy(a_in, a_in, as_s.at[c], as_r.at[c], sibling).wait_recv()
        if c == 0:
            weights[0].wait()
        dot_in(c, wg, pg, sg)
        x_copy(c, 0).start()
        x_copy(c, 1).start()

    def m_up(c):
        if c == 0:
            weights[1].wait()
        dot_in(c, wu, pu, su)
        x_copy(c, 2).start()
        x_copy(c, 3).start()

    def rows(q):
        return pl.ds(pl.multiple_of(q * Q, Q), Q)

    def r_gate(c):
        x_recv(c, 0)
        mg[c] = (pg[c, rows(xp), :] + r1g[c].astype(F32)).astype(BF16)
        x_copy(c, 4).start()

    def r_up(c):
        x_recv(c, 3)
        mu[c] = (pu[c, rows(xm), :] + r1u[c].astype(F32)).astype(BF16)
        x_copy(c, 5).start()

    def act(c):
        x_recv(c, 1)
        x_recv(c, 2)
        x_recv(c, 4)
        x_recv(c, 5)
        gate = pg[c, rows(x), :] + rmg[c].astype(F32) + rpg[c].astype(F32)
        up = pu[c, rows(x), :] + rmu[c].astype(F32) + rpu[c].astype(F32)
        hb[c, x] = (gate / (1.0 + jnp.exp(-gate)) * up).astype(BF16)
        x_copy(c, 6).start()
        x_copy(c, 7).start()

    def forward(c):
        x_recv(c, 6)
        x_copy(c, 8).start()
        x_recv(c, 7)
        x_copy(c, 9).start()

    def d0(c):
        return rcopy(ob.at[c, :, 1 - k], sib.at[c], d0_s.at[c], d0_r.at[c], sibling)

    def m2(c):
        x_recv(c, 8)
        x_recv(c, 9)
        if c == 0:
            weights[2].wait()

        n = DL // 2
        for j in range(2):
            r = jnp.dot(hb[c].reshape(T, FL), wd[:, j * n:(j + 1) * n], preferred_element_type=F32)
            r = r.T.reshape(CH // 2, 2, NB, T)
            of[c % 2, j * CH // 2:(j + 1) * CH // 2] = r
            ob[c, j * CH // 2:(j + 1) * CH // 2] = r.astype(BF16)
        d0(c).start()

    def scatter(c):
        d0(c).wait_recv()
        sd[c] = (of[c % 2, :, k] + sib[c].astype(F32)).astype(BF16)
        sf[c] = of[c % 2, chip, k] + sib[c, chip].astype(F32)

        def one(o, _):
            q = peer(o)
            rcopy(sd.at[c, q], rd.at[c, o - 1], d1_s.at[c], d1_r.at[c], (x, q * 2 + k)).start()
            return 0
        lax.fori_loop(1, CH, one, 0)

    def d1_all(c):
        return rcopy(rd.at[c], rd.at[c], d1_s.at[c], d1_r.at[c], sibling)

    def finish(c):
        d1_all(c).wait_recv()
        total = sf[c]
        for o in range(CH - 1):
            total = total + rd[c, o].astype(F32)
        out[:, c * T:(c + 1) * T] = total.astype(BF16)

    order = (
        (a_send, 0), (a_send, 1), (a_send, 2), (to_sibling, 0), (m_gate, 0), (m_up, 0), (to_sibling, 1), (a_send, 3),
        (m_gate, 1), (r_gate, 0), (m_up, 1), (r_up, 0), (to_sibling, 2), (m_gate, 2), (r_gate, 1), (r_up, 1), (m_up, 2),
        (act, 0), (act, 1), (to_sibling, 3), (r_gate, 2), (r_up, 2), (forward, 0), (m_gate, 3), (m_up, 3),
        (act, 2), (forward, 1), (m2, 0), (r_gate, 3), (r_up, 3), (scatter, 0), (forward, 2), (m2, 1), (act, 3),
        (scatter, 1), (m2, 2), (forward, 3), (scatter, 2), (m2, 3), (scatter, 3),
        (finish, 0), (finish, 1), (finish, 2), (finish, 3),
    )
    for step, c in order:
        step(c)

    for c in range(NC):
        a_all(c).wait_send()
        a_pass(c).wait_send()
        for i in range(10):
            x_copy(c, i).wait_send()
        d0(c).wait_send()
        d1_all(c).wait_send()


def body(tokens, gate_weight, up_weight, down_weight):
    vm = pltpu.VMEM
    dma = pltpu.SemaphoreType.DMA
    return pl.pallas_call(
        kernel,
        out_shape=jax.ShapeDtypeStruct((NB, TOK), BF16),
        in_specs=[pl.BlockSpec(memory_space=pltpu.VMEM)] + [pl.BlockSpec(memory_space=pl.ANY)] * 3,
        out_specs=pl.BlockSpec(memory_space=pltpu.VMEM),
        scratch_shapes=[
            vm((DL, FL), BF16), vm((DL, FL), BF16), vm((FL, DL), BF16),
            vm((NC, CH, 2, NB, T), BF16),
            vm((NC, T, FL), F32), vm((NC, T, FL), F32),
            vm((NC, 4, Q, FL), BF16), vm((NC, 4, Q, FL), BF16),
            vm((NC, Q, FL), BF16), vm((NC, Q, FL), BF16),
            vm((NC, Q, FL), BF16), vm((NC, Q, FL), BF16),
            vm((NC, Q, FL), BF16), vm((NC, Q, FL), BF16),
            vm((NC, Q, FL), BF16), vm((NC, Q, FL), BF16),
            vm((NC, 4, Q, FL), BF16),
            vm((NC, CH, 2, NB, T), BF16), vm((2, CH, 2, NB, T), F32),
            vm((NC, CH, NB, T), BF16), vm((NC, CH, NB, T), BF16),
            vm((NC, NB, T), F32), vm((NC, CH - 1, NB, T), BF16),
            dma((3,)), dma((NC,)), dma((NC,)), dma((NC,)), dma((NC,)),
            dma((NC, 10)), dma((NC, 10)), dma((NC,)), dma((NC,)), dma((NC,)), dma((NC,)),
        ],
        compiler_params=pltpu.CompilerParams(
            collective_id=0, has_side_effects=True, vmem_limit_bytes=60 * 2 ** 20
        ),
        cost_estimate=pl.CostEstimate(flops=12 * 10 ** 9, bytes_accessed=24 * 10 ** 6, transcendentals=0),
    )(tokens.T, gate_weight, up_weight, down_weight).T


def solution(mesh):
    return jax.shard_map(
        body,
        mesh=mesh,
        in_specs=(P(None, ("gx", "yz")), P("gx", "yz"), P("gx", "yz"), P("yz", "gx")),
        out_specs=P(None, ("gx", "yz")),
        check_vma=False,
    )
```

```python
import jax
import jax.numpy as jnp
from jax import lax
from jax.experimental import pallas as pl
from jax.experimental.pallas import tpu as pltpu
from jax.sharding import PartitionSpec as P

MESH = pl.DeviceIdType.MESH
F32 = jnp.float32
BF16 = jnp.bfloat16

TOK = 512
NC = 4
T = TOK // NC
Q = T // 4
DL = 3072
FL = 1280
NB = 96
CH = 16
ROW = 4 * 2 * NB

PARTS = (((0, 1280),), ((0, 1280),), ((0, 1280),), ((0, 768), (768, 512)))
MAXP = max(len(p) for p in PARTS)
STRAIGHT = (3,)


def kernel(tok, wg_h, wu_h, wd_h, out,
           wg, wu, wd, xt, pg, pu, sg, su, r1g, r1u, mg, mu, rmg, rmu, rpg, rpu,
           hb, ob, of, sib, sd, sf, rd, ot,
           wsem, t_s, o_s, a_s, a_r, as_s, as_r, x_s, x_r, d0_s, d0_r, d1_s, d1_r):
    x = lax.axis_index("gx")
    yz = lax.axis_index("yz")
    chip = yz // 2
    k = yz % 2
    y = chip // 4
    z = chip % 4
    xp = (x + 1) % 4
    xm = (x + 3) % 4
    xo = (x + 2) % 4
    sibling = (x, chip * 2 + (1 - k))
    plus = (xp, yz)
    minus = (xm, yz)
    opposite = (xo, yz)

    def peer(dy, dz):
        return ((y + dy) % 4) * 4 + (z + dz) % 4

    far_first = [(dy, dz) for dy in (2, 1, 3, 0) for dz in (2, 1, 3, 0) if dy or dz]
    far_first.sort(key=lambda d: -min(d[0], 4 - d[0]) - min(d[1], 4 - d[1]))

    barrier = pltpu.get_barrier_semaphore()
    for dy, dz in far_first:
        pl.semaphore_signal(barrier, inc=1, device_id=(x, peer(dy, dz) * 2 + k), device_id_type=MESH)
    for dev in (opposite, plus, minus, sibling):
        pl.semaphore_signal(barrier, inc=1, device_id=dev, device_id_type=MESH)

    own_tokens = [pltpu.make_async_copy(tok.at[:, pl.ds(c * T, T)], xt.at[c, k, chip], t_s.at[c]) for c in range(NC)]
    weights = [pltpu.make_async_copy(h, v, wsem.at[i]) for i, (h, v) in enumerate(((wg_h, wg), (wu_h, wu), (wd_h, wd)))]
    for copy in own_tokens + weights:
        copy.start()

    pl.semaphore_wait(barrier, CH - 1 + 4)

    def rcopy(src, dst, ss, rs, dev):
        return pltpu.make_async_remote_copy(src_ref=src, dst_ref=dst, send_sem=ss, recv_sem=rs,
                                            device_id=dev, device_id_type=MESH)

    pending = []

    def start(copy):
        copy.start()
        pending.append(copy)

    def a_send(c):
        own_tokens[c].wait()
        own = xt.at[c, k, chip]
        for dy, dz in far_first:
            rcopy(own, own, a_s.at[c], a_r.at[c], (x, peer(dy, dz) * 2 + k)).start()
        pending.append(a_all(c))

    def a_all(c):
        ref = xt.at[c, k, pl.ds(0, CH - 1)]
        return rcopy(ref, ref, a_s.at[c], a_r.at[c], sibling)

    def a_pass(c):
        ref = xt.at[c, k]
        return rcopy(ref, ref, as_s.at[c], as_r.at[c], sibling)

    def to_sibling(c):
        a_all(c).wait_recv()
        start(a_pass(c))

    def x_copy(c, p, i):
        s, w = PARTS[c][p]
        cols = pl.ds(s, w)
        hx = hb.at[c, x, :, cols]
        if i == 8 and c in STRAIGHT:
            src, dst, dev = hx, hx, opposite
        else:
            lo = hb.at[c, xm, pl.ds(0, Q // 2), cols]
            hi = hb.at[c, xp, pl.ds(Q // 2, Q // 2), cols]
            src, dst, dev = (
                (sg.at[c, xo, :, cols], r1g.at[c, :, cols], plus),
                (sg.at[c, xm, :, cols], rpg.at[c, :, cols], minus),
                (su.at[c, xp, :, cols], rmu.at[c, :, cols], plus),
                (su.at[c, xo, :, cols], r1u.at[c, :, cols], minus),
                (mg.at[c, :, cols], rmg.at[c, :, cols], plus),
                (mu.at[c, :, cols], rpu.at[c, :, cols], minus),
                (hx, hx, plus),
                (hx, hx, minus),
                (lo, lo, plus),
                (hi, hi, minus),
            )[i]
        return rcopy(src, dst, x_s.at[c, p, i], x_r.at[c, p, i], dev)

    def x_recv(c, p, i):
        s, w = PARTS[c][p]
        cols = pl.ds(s, w)
        if i == 8 and c in STRAIGHT:
            dst = hb.at[c, xo, :, cols]
        else:
            dst = (r1g.at[c, :, cols], rpg.at[c, :, cols], rmu.at[c, :, cols], r1u.at[c, :, cols],
                   rmg.at[c, :, cols], rpu.at[c, :, cols], hb.at[c, xm, :, cols], hb.at[c, xp, :, cols],
                   hb.at[c, xo, pl.ds(0, Q // 2), cols], hb.at[c, xo, pl.ds(Q // 2, Q // 2), cols])[i]
        rcopy(dst, dst, x_s.at[c, p, i], x_r.at[c, p, i], plus).wait_recv()

    def dot_in(c, core, w, s, n):
        return lax.dot_general(xt[c, core].reshape(DL // 2, T), w[:, core, :, s:s + n].reshape(DL // 2, n),
                               (((0,), (0,)), ((), ())), preferred_element_type=F32)

    def m_own(c):
        if c == 0:
            weights[0].wait()
        pg[c] = dot_in(c, k, wg, 0, FL)
        if c == 0:
            weights[1].wait()
        pu[c] = dot_in(c, k, wu, 0, FL)

    def m_gate(c, p):
        if p == 0:
            a_in = xt.at[c, 1 - k]
            rcopy(a_in, a_in, as_s.at[c], as_r.at[c], sibling).wait_recv()
        s, n = PARTS[c][p]
        r = pg[c, :, s:s + n] + dot_in(c, 1 - k, wg, s, n)
        pg[c, :, s:s + n] = r
        sg[c, :, :, s:s + n] = r.astype(BF16).reshape(4, Q, n)
        start(x_copy(c, p, 0))
        start(x_copy(c, p, 1))

    def m_up(c, p):
        s, n = PARTS[c][p]
        r = pu[c, :, s:s + n] + dot_in(c, 1 - k, wu, s, n)
        pu[c, :, s:s + n] = r
        su[c, :, :, s:s + n] = r.astype(BF16).reshape(4, Q, n)
        start(x_copy(c, p, 2))
        start(x_copy(c, p, 3))

    def rows(q):
        return pl.ds(pl.multiple_of(q * Q, Q), Q)

    def r_gate(c, p):
        s, n = PARTS[c][p]
        x_recv(c, p, 0)
        mg[c, :, s:s + n] = (pg[c, rows(xp), s:s + n] + r1g[c, :, s:s + n].astype(F32)).astype(BF16)
        start(x_copy(c, p, 4))

    def r_up(c, p):
        s, n = PARTS[c][p]
        x_recv(c, p, 3)
        mu[c, :, s:s + n] = (pu[c, rows(xm), s:s + n] + r1u[c, :, s:s + n].astype(F32)).astype(BF16)
        start(x_copy(c, p, 5))

    def act(c, p):
        s, n = PARTS[c][p]
        for i in (1, 2, 4, 5):
            x_recv(c, p, i)
        gate = pg[c, rows(x), s:s + n] + rmg[c, :, s:s + n].astype(F32) + rpg[c, :, s:s + n].astype(F32)
        up = pu[c, rows(x), s:s + n] + rmu[c, :, s:s + n].astype(F32) + rpu[c, :, s:s + n].astype(F32)
        hb[c, x, :, s:s + n] = (gate / (1.0 + jnp.exp(-gate)) * up).astype(BF16)
        for i in (8, 6, 7) if c in STRAIGHT else (6, 7):
            start(x_copy(c, p, i))

    def forward(c, p):
        if c not in STRAIGHT:
            x_recv(c, p, 6)
            start(x_copy(c, p, 8))
            x_recv(c, p, 7)
            start(x_copy(c, p, 9))

    halves = ((2, 0), (1, 3))

    def d0(c, dy):
        chips = pl.ds(4 * ((y + dy) % 4), 4)
        return rcopy(ob.at[c, 1 - k, chips], sib.at[c, chips], d0_s.at[c, dy], d0_r.at[c, dy], sibling)

    def m2(c, j):
        if j == 0:
            for p in range(len(PARTS[c])):
                for i in (6, 7, 8) if c in STRAIGHT else (8, 9):
                    x_recv(c, p, i)
            if c == 0:
                weights[2].wait()
        for dy in halves[j]:
            yd = (y + dy) % 4
            cols = pl.ds(pl.multiple_of(yd * ROW, ROW), ROW)
            r = jnp.dot(hb[c].reshape(T, FL), wd[:, cols], preferred_element_type=F32)
            r = r.T.reshape(4, 2, NB, T)
            chips = pl.ds(4 * yd, 4)
            for core in range(2):
                of[c % 2, core, chips] = r[:, core]
                ob[c, core, chips] = r[:, core].astype(BF16)
            start(d0(c, dy))

    def scatter(c, j):
        for dy in halves[j]:
            d0(c, dy).wait_recv()
            chips = pl.ds(4 * ((y + dy) % 4), 4)
            sd[c, chips] = (of[c % 2, k, chips] + sib[c, chips].astype(F32)).astype(BF16)
            if dy == 0:
                sf[c] = of[c % 2, k, chip] + sib[c, chip].astype(F32)
            for dz in (2, 1, 3, 0):
                if dy or dz:
                    q = peer(dy, dz)
                    rcopy(sd.at[c, q], rd.at[c, 4 * dy + dz - 1], d1_s.at[c], d1_r.at[c], (x, q * 2 + k)).start()
        if j == 1:
            pending.append(d1_all(c))

    def d1_all(c):
        return rcopy(rd.at[c], rd.at[c], d1_s.at[c], d1_r.at[c], sibling)

    def finish(c):
        d1_all(c).wait_recv()
        total = sf[c]
        for o in range(CH - 1):
            total = total + rd[c, o].astype(F32)
        ot[c] = total.astype(BF16)
        done = pltpu.make_async_copy(ot.at[c], out.at[:, pl.ds(c * T, T)], o_s.at[c])
        done.start()
        finished.append(done)

    finished = []
    order = (
        (a_send, 0), (a_send, 1), (a_send, 2), (to_sibling, 0), (m_own, 0), (m_gate, 0, 0), (m_up, 0, 0),
        (to_sibling, 1), (m_own, 1), (m_gate, 1, 0), (a_send, 3), (m_up, 1, 0), (r_gate, 0, 0), (r_up, 0, 0),
        (to_sibling, 2), (m_own, 2), (m_gate, 2, 0), (r_gate, 1, 0), (r_up, 1, 0), (to_sibling, 3), (act, 0, 0),
        (m_up, 2, 0), (m_own, 3), (m_gate, 3, 0), (forward, 0, 0), (act, 1, 0), (r_gate, 2, 0), (r_up, 2, 0),
        (m_up, 3, 0), (m2, 0, 0), (forward, 1, 0), (m_gate, 3, 1), (m_up, 3, 1), (m2, 0, 1), (act, 2, 0),
        (scatter, 0, 0), (scatter, 0, 1), (r_gate, 3, 0), (r_up, 3, 0), (r_up, 3, 1), (r_gate, 3, 1), (m2, 1, 0),
        (forward, 2, 0), (m2, 1, 1), (act, 3, 0), (scatter, 1, 0), (scatter, 1, 1), (act, 3, 1), (m2, 2, 0),
        (m2, 2, 1), (scatter, 2, 0), (scatter, 2, 1), (m2, 3, 0), (m2, 3, 1), (scatter, 3, 0), (finish, 1),
        (scatter, 3, 1), (finish, 2), (finish, 0), (finish, 3),
    )
    for step, *where in order:
        step(*where)

    for copy in pending:
        copy.wait_send()
    for copy in finished:
        copy.wait()


def body(tokens, gate_weight, up_weight, down_weight):
    vm = pltpu.VMEM
    dma = pltpu.SemaphoreType.DMA
    return pl.pallas_call(
        kernel,
        out_shape=jax.ShapeDtypeStruct((NB, TOK), BF16),
        in_specs=[pl.BlockSpec(memory_space=pl.ANY)] * 4,
        out_specs=pl.BlockSpec(memory_space=pl.ANY),
        scratch_shapes=[
            vm((CH, 2, NB, FL), BF16), vm((CH, 2, NB, FL), BF16), vm((FL, DL), BF16),
            vm((NC, 2, CH, NB, T), BF16),
            vm((NC, T, FL), F32), vm((NC, T, FL), F32),
            vm((NC, 4, Q, FL), BF16), vm((NC, 4, Q, FL), BF16),
            vm((NC, Q, FL), BF16), vm((NC, Q, FL), BF16),
            vm((NC, Q, FL), BF16), vm((NC, Q, FL), BF16),
            vm((NC, Q, FL), BF16), vm((NC, Q, FL), BF16),
            vm((NC, Q, FL), BF16), vm((NC, Q, FL), BF16),
            vm((NC, 4, Q, FL), BF16),
            vm((NC, 2, CH, NB, T), BF16), vm((2, 2, CH, NB, T), F32),
            vm((NC, CH, NB, T), BF16), vm((NC, CH, NB, T), BF16),
            vm((NC, NB, T), F32), vm((NC, CH - 1, NB, T), BF16), vm((NC, NB, T), BF16),
            dma((3,)), dma((NC,)), dma((NC,)), dma((NC,)), dma((NC,)), dma((NC,)), dma((NC,)),
            dma((NC, MAXP, 10)), dma((NC, MAXP, 10)), dma((NC, 4)), dma((NC, 4)), dma((NC,)), dma((NC,)),
        ],
        compiler_params=pltpu.CompilerParams(
            collective_id=0, has_side_effects=True, vmem_limit_bytes=60 * 2 ** 20
        ),
        cost_estimate=pl.CostEstimate(flops=12 * 10 ** 9, bytes_accessed=24 * 10 ** 6, transcendentals=0),
    )(tokens.T, gate_weight.reshape(CH, 2, NB, FL), up_weight.reshape(CH, 2, NB, FL), down_weight).T


def solution(mesh):
    return jax.shard_map(
        body,
        mesh=mesh,
        in_specs=(P(None, ("gx", "yz")), P("gx", "yz"), P("gx", "yz"), P("yz", "gx")),
        out_specs=P(None, ("gx", "yz")),
        check_vma=False,
    )
```

```python
import jax
import jax.numpy as jnp
from jax import lax
from jax.experimental import pallas as pl
from jax.experimental.pallas import tpu as pltpu
from jax.sharding import PartitionSpec as P

MESH = pl.DeviceIdType.MESH
F32 = jnp.float32
BF16 = jnp.bfloat16

TOK = 512
NC = 4
T = TOK // NC
Q = T // 4
DL = 3072
FL = 1280
NB = 96
CH = 16
ROW = 4 * 2 * NB

PARTS = (((0, 1280),), ((0, 1280),), ((0, 1280),), ((0, 768), (768, 512)))
MAXP = max(len(p) for p in PARTS)
STRAIGHT = (3,)


def kernel(tok, wg_h, wu_h, wd_h, out,
           wg, wu, wd, xt, pg, pu, sg, su, r1g, r1u, mg, mu, rmg, rmu, rpg, rpu,
           hb, ob, of, sib, sd, sf, rd, ot,
           wsem, t_s, o_s, a_s, a_r, as_s, as_r, x_s, x_r, d0_s, d0_r, d1_s, d1_r):
    x = lax.axis_index("gx")
    yz = lax.axis_index("yz")
    chip = yz // 2
    k = yz % 2
    y = chip // 4
    z = chip % 4
    xp = (x + 1) % 4
    xm = (x + 3) % 4
    xo = (x + 2) % 4
    sibling = (x, chip * 2 + (1 - k))
    plus = (xp, yz)
    minus = (xm, yz)
    opposite = (xo, yz)

    row = [y] + [(y + d) % 4 for d in (1, 2, 3)]
    col = [z] + [(z + d) % 4 for d in (1, 2, 3)]
    peer = [[(x, row[dy] * 8 + col[dz] * 2 + k) for dz in range(4)] for dy in range(4)]

    far_first = [(dy, dz) for dy in (2, 1, 3, 0) for dz in (2, 1, 3, 0) if dy or dz]
    far_first.sort(key=lambda d: -min(d[0], 4 - d[0]) - min(d[1], 4 - d[1]))

    barrier = pltpu.get_barrier_semaphore()
    for dy, dz in far_first:
        pl.semaphore_signal(barrier, inc=1, device_id=peer[dy][dz], device_id_type=MESH)
    for dev in (opposite, plus, minus, sibling):
        pl.semaphore_signal(barrier, inc=1, device_id=dev, device_id_type=MESH)

    own_tokens = [pltpu.make_async_copy(tok.at[:, pl.ds(c * T, T)], xt.at[c, k, chip], t_s.at[c]) for c in range(NC)]
    weights = [pltpu.make_async_copy(h, v, wsem.at[i]) for i, (h, v) in enumerate(((wg_h, wg), (wu_h, wu), (wd_h, wd)))]
    for copy in own_tokens + weights:
        copy.start()

    pl.semaphore_wait(barrier, CH - 1 + 4)

    def rcopy(src, dst, ss, rs, dev):
        return pltpu.make_async_remote_copy(src_ref=src, dst_ref=dst, send_sem=ss, recv_sem=rs,
                                            device_id=dev, device_id_type=MESH)

    pending = []

    def start(copy):
        copy.start()
        pending.append(copy)

    def a_send(c):
        own_tokens[c].wait()
        own = xt.at[c, k, chip]
        for dy, dz in far_first:
            rcopy(own, own, a_s.at[c], a_r.at[c], peer[dy][dz]).start()
        pending.append(a_all(c))

    def a_all(c):
        ref = xt.at[c, k, pl.ds(0, CH - 1)]
        return rcopy(ref, ref, a_s.at[c], a_r.at[c], sibling)

    def a_pass(c):
        ref = xt.at[c, k]
        return rcopy(ref, ref, as_s.at[c], as_r.at[c], sibling)

    def to_sibling(c):
        a_all(c).wait_recv()
        start(a_pass(c))

    def x_copy(c, p, i):
        s, w = PARTS[c][p]
        cols = pl.ds(s, w)
        hx = hb.at[c, x, :, cols]
        if i == 8 and c in STRAIGHT:
            src, dst, dev = hx, hx, opposite
        else:
            lo = hb.at[c, xm, pl.ds(0, Q // 2), cols]
            hi = hb.at[c, xp, pl.ds(Q // 2, Q // 2), cols]
            src, dst, dev = (
                (sg.at[c, xo, :, cols], r1g.at[c, :, cols], plus),
                (sg.at[c, xm, :, cols], rpg.at[c, :, cols], minus),
                (su.at[c, xp, :, cols], rmu.at[c, :, cols], plus),
                (su.at[c, xo, :, cols], r1u.at[c, :, cols], minus),
                (mg.at[c, :, cols], rmg.at[c, :, cols], plus),
                (mu.at[c, :, cols], rpu.at[c, :, cols], minus),
                (hx, hx, plus),
                (hx, hx, minus),
                (lo, lo, plus),
                (hi, hi, minus),
            )[i]
        return rcopy(src, dst, x_s.at[c, p, i], x_r.at[c, p, i], dev)

    def x_recv(c, p, i):
        s, w = PARTS[c][p]
        cols = pl.ds(s, w)
        if i == 8 and c in STRAIGHT:
            dst = hb.at[c, xo, :, cols]
        else:
            dst = (r1g.at[c, :, cols], rpg.at[c, :, cols], rmu.at[c, :, cols], r1u.at[c, :, cols],
                   rmg.at[c, :, cols], rpu.at[c, :, cols], hb.at[c, xm, :, cols], hb.at[c, xp, :, cols],
                   hb.at[c, xo, pl.ds(0, Q // 2), cols], hb.at[c, xo, pl.ds(Q // 2, Q // 2), cols])[i]
        rcopy(dst, dst, x_s.at[c, p, i], x_r.at[c, p, i], plus).wait_recv()

    def dot_in(c, core, w, s, n):
        return lax.dot_general(xt[c, core].reshape(DL // 2, T), w[:, core, :, s:s + n].reshape(DL // 2, n),
                               (((0,), (0,)), ((), ())), preferred_element_type=F32)

    def m_own(c):
        if c == 0:
            weights[0].wait()
        pg[c] = dot_in(c, k, wg, 0, FL)
        if c == 0:
            weights[1].wait()
        pu[c] = dot_in(c, k, wu, 0, FL)

    def m_gate(c, p):
        if p == 0:
            a_in = xt.at[c, 1 - k]
            rcopy(a_in, a_in, as_s.at[c], as_r.at[c], sibling).wait_recv()
        s, n = PARTS[c][p]
        r = pg[c, :, s:s + n] + dot_in(c, 1 - k, wg, s, n)
        pg[c, :, s:s + n] = r
        sg[c, :, :, s:s + n] = r.astype(BF16).reshape(4, Q, n)
        start(x_copy(c, p, 0))
        start(x_copy(c, p, 1))

    def m_up(c, p):
        s, n = PARTS[c][p]
        r = pu[c, :, s:s + n] + dot_in(c, 1 - k, wu, s, n)
        pu[c, :, s:s + n] = r
        su[c, :, :, s:s + n] = r.astype(BF16).reshape(4, Q, n)
        start(x_copy(c, p, 2))
        start(x_copy(c, p, 3))

    def rows(q):
        return pl.ds(pl.multiple_of(q * Q, Q), Q)

    def r_gate(c, p):
        s, n = PARTS[c][p]
        x_recv(c, p, 0)
        mg[c, :, s:s + n] = (pg[c, rows(xp), s:s + n] + r1g[c, :, s:s + n].astype(F32)).astype(BF16)
        start(x_copy(c, p, 4))

    def r_up(c, p):
        s, n = PARTS[c][p]
        x_recv(c, p, 3)
        mu[c, :, s:s + n] = (pu[c, rows(xm), s:s + n] + r1u[c, :, s:s + n].astype(F32)).astype(BF16)
        start(x_copy(c, p, 5))

    def act(c, p):
        s, n = PARTS[c][p]
        for i in (1, 2, 4, 5):
            x_recv(c, p, i)
        gate = pg[c, rows(x), s:s + n] + rmg[c, :, s:s + n].astype(F32) + rpg[c, :, s:s + n].astype(F32)
        up = pu[c, rows(x), s:s + n] + rmu[c, :, s:s + n].astype(F32) + rpu[c, :, s:s + n].astype(F32)
        hb[c, x, :, s:s + n] = (gate / (1.0 + jnp.exp(-gate)) * up).astype(BF16)
        for i in (8, 6, 7) if c in STRAIGHT else (6, 7):
            start(x_copy(c, p, i))

    def forward(c, p):
        if c not in STRAIGHT:
            x_recv(c, p, 6)
            start(x_copy(c, p, 8))
            x_recv(c, p, 7)
            start(x_copy(c, p, 9))

    halves = ((2, 0), (1, 3))

    def d0(c, dy):
        chips = pl.ds(4 * ((y + dy) % 4), 4)
        return rcopy(ob.at[c, 1 - k, chips], sib.at[c, chips], d0_s.at[c, dy], d0_r.at[c, dy], sibling)

    def m2(c, j):
        if j == 0:
            for p in range(len(PARTS[c])):
                for i in (6, 7, 8) if c in STRAIGHT else (8, 9):
                    x_recv(c, p, i)
            if c == 0:
                weights[2].wait()
        for dy in halves[j]:
            yd = (y + dy) % 4
            cols = pl.ds(pl.multiple_of(yd * ROW, ROW), ROW)
            r = jnp.dot(hb[c].reshape(T, FL), wd[:, cols], preferred_element_type=F32)
            r = r.T.reshape(4, 2, NB, T)
            chips = pl.ds(4 * yd, 4)
            for core in range(2):
                of[c % 2, core, chips] = r[:, core]
                ob[c, core, chips] = r[:, core].astype(BF16)
            start(d0(c, dy))

    def scatter(c, j):
        for dy in halves[j]:
            d0(c, dy).wait_recv()
            chips = pl.ds(4 * ((y + dy) % 4), 4)
            sd[c, chips] = (of[c % 2, k, chips] + sib[c, chips].astype(F32)).astype(BF16)
        for dz in (2, 1, 3, 0):
            for dy in halves[j]:
                if dy or dz:
                    q = row[dy] * 4 + col[dz]
                    rcopy(sd.at[c, q], rd.at[c, 4 * dy + dz - 1], d1_s.at[c], d1_r.at[c], peer[dy][dz]).start()
        if j == 0:
            sf[c] = of[c % 2, k, chip] + sib[c, chip].astype(F32)
        else:
            pending.append(d1_all(c))

    def d1_all(c):
        return rcopy(rd.at[c], rd.at[c], d1_s.at[c], d1_r.at[c], sibling)

    def finish(c):
        d1_all(c).wait_recv()
        total = sf[c]
        for o in range(CH - 1):
            total = total + rd[c, o].astype(F32)
        ot[c] = total.astype(BF16)
        done = pltpu.make_async_copy(ot.at[c], out.at[:, pl.ds(c * T, T)], o_s.at[c])
        done.start()
        finished.append(done)

    finished = []
    order = (
        (a_send, 0), (a_send, 1), (to_sibling, 0), (a_send, 2), (m_own, 0), (m_gate, 0, 0), (m_up, 0, 0),
        (to_sibling, 1), (m_own, 1), (m_gate, 1, 0), (a_send, 3), (m_up, 1, 0), (r_gate, 0, 0), (r_up, 0, 0),
        (to_sibling, 2), (m_own, 2), (m_gate, 2, 0), (r_gate, 1, 0), (r_up, 1, 0), (to_sibling, 3), (act, 0, 0),
        (m_up, 2, 0), (m_own, 3), (m_gate, 3, 0), (forward, 0, 0), (act, 1, 0), (r_gate, 2, 0), (r_up, 2, 0),
        (m_up, 3, 0), (m2, 0, 0), (forward, 1, 0), (m_gate, 3, 1), (m_up, 3, 1), (m2, 0, 1), (act, 2, 0),
        (scatter, 0, 0), (scatter, 0, 1), (r_gate, 3, 0), (r_up, 3, 0), (r_up, 3, 1), (r_gate, 3, 1), (m2, 1, 0),
        (forward, 2, 0), (m2, 1, 1), (act, 3, 0), (scatter, 1, 0), (scatter, 1, 1), (act, 3, 1), (m2, 2, 0),
        (m2, 2, 1), (scatter, 2, 0), (scatter, 2, 1), (m2, 3, 0), (m2, 3, 1), (scatter, 3, 0), (finish, 1),
        (scatter, 3, 1), (finish, 2), (finish, 0), (finish, 3),
    )
    for step, *where in order:
        step(*where)

    for copy in pending:
        copy.wait_send()
    for copy in finished:
        copy.wait()


def body(tokens, gate_weight, up_weight, down_weight):
    vm = pltpu.VMEM
    dma = pltpu.SemaphoreType.DMA
    return pl.pallas_call(
        kernel,
        out_shape=jax.ShapeDtypeStruct((NB, TOK), BF16),
        in_specs=[pl.BlockSpec(memory_space=pl.ANY)] * 4,
        out_specs=pl.BlockSpec(memory_space=pl.ANY),
        scratch_shapes=[
            vm((CH, 2, NB, FL), BF16), vm((CH, 2, NB, FL), BF16), vm((FL, DL), BF16),
            vm((NC, 2, CH, NB, T), BF16),
            vm((NC, T, FL), F32), vm((NC, T, FL), F32),
            vm((NC, 4, Q, FL), BF16), vm((NC, 4, Q, FL), BF16),
            vm((NC, Q, FL), BF16), vm((NC, Q, FL), BF16),
            vm((NC, Q, FL), BF16), vm((NC, Q, FL), BF16),
            vm((NC, Q, FL), BF16), vm((NC, Q, FL), BF16),
            vm((NC, Q, FL), BF16), vm((NC, Q, FL), BF16),
            vm((NC, 4, Q, FL), BF16),
            vm((NC, 2, CH, NB, T), BF16), vm((2, 2, CH, NB, T), F32),
            vm((NC, CH, NB, T), BF16), vm((NC, CH, NB, T), BF16),
            vm((NC, NB, T), F32), vm((NC, CH - 1, NB, T), BF16), vm((NC, NB, T), BF16),
            dma((3,)), dma((NC,)), dma((NC,)), dma((NC,)), dma((NC,)), dma((NC,)), dma((NC,)),
            dma((NC, MAXP, 10)), dma((NC, MAXP, 10)), dma((NC, 4)), dma((NC, 4)), dma((NC,)), dma((NC,)),
        ],
        compiler_params=pltpu.CompilerParams(
            collective_id=0, has_side_effects=True, vmem_limit_bytes=60 * 2 ** 20
        ),
        cost_estimate=pl.CostEstimate(flops=12 * 10 ** 9, bytes_accessed=24 * 10 ** 6, transcendentals=0),
    )(tokens.T, gate_weight.reshape(CH, 2, NB, FL), up_weight.reshape(CH, 2, NB, FL), down_weight).T


def solution(mesh):
    return jax.shard_map(
        body,
        mesh=mesh,
        in_specs=(P(None, ("gx", "yz")), P("gx", "yz"), P("gx", "yz"), P("yz", "gx")),
        out_specs=P(None, ("gx", "yz")),
        check_vma=False,
    )
```
